256 devices in a mesh: pipe: 64 (over x, y, z_hi, core), dp: 4 (over z_lo).
Axes of the slice: x: 4, y: 4, z: 8 (z_hi: 2, z_lo: 4; z = z_hi * 4 + z_lo), core: 2. Of those that a mesh axis runs over, the one named last changes fastest.
Arguments:
- lead_front: bfloat16 [64, 512, 3072], P('pipe', 'dp'), may hold values from -19 to 19
- mirror_front: bfloat16 [64, 512, 3072], P('pipe', 'dp'), may hold values from -19 to 19
- lead_grad: bfloat16 [64, 512, 3072], P('pipe', 'dp'), may hold values from -19 to 19
- mirror_grad: bfloat16 [64, 512, 3072], P('pipe', 'dp'), may hold values from -19 to 19
- lead_saved: bfloat16 [64, 2, 512, 3072], P('pipe', None, 'dp'), may hold values from -19 to 19
- mirror_saved: bfloat16 [64, 2, 512, 3072], P('pipe', None, 'dp'), may hold values from -19 to 19
- lead_down: bfloat16 [64, 3072, 256], P('pipe', 'dp'), may hold values from -0.109375 to 0.109375
- lead_up: bfloat16 [64, 256, 3072], P('pipe', None, 'dp'), may hold values from -0.375 to 0.375
- mirror_down: bfloat16 [64, 3072, 256], P('pipe', 'dp'), may hold values from -0.109375 to 0.109375
- mirror_up: bfloat16 [64, 256, 3072], P('pipe', None, 'dp'), may hold values from -0.375 to 0.375
Outputs:
- lead_out: bfloat16 [64, 512, 3072], P('pipe', 'dp')
- mirror_out: bfloat16 [64, 512, 3072], P('pipe', 'dp')
- lead_dx: bfloat16 [64, 512, 3072], P('pipe', 'dp')
- mirror_dx: bfloat16 [64, 512, 3072], P('pipe', 'dp')
- lead_down_grad: bfloat16 [64, 3072, 256], P('pipe', 'dp')
- lead_up_grad: bfloat16 [64, 256, 3072], P('pipe', None, 'dp')
- mirror_down_grad: bfloat16 [64, 3072, 256], P('pipe', 'dp')
- mirror_up_grad: bfloat16 [64, 256, 3072], P('pipe', None, 'dp')
The draws below stay inside these ranges and needn't reach their ends.
All inputs are finite; a program needn't handle non-finite values.
Results may differ from the reference program's by a relative error of at most 0.013.
Values may be sent and summed in bfloat16 or wider, within the bound.
A program may use at most 128 MiB of HBM per device.

```python
import math
import jax
import jax.numpy as jnp
from jax import lax

D = 3072
R = 256
TICKS = 2
SECTIONS = 64
TOKENS = 512


def make_field(key, lead_shape):
    subkeys = jax.random.split(key, 5)
    full_shape = lead_shape + (D,)
    gaussian = jnp.clip(jax.random.normal(subkeys[0], full_shape, jnp.float32), -4.0, 4.0)
    columns = jnp.exp(jax.random.uniform(subkeys[3], (D,), jnp.float32, 0.0, math.log(10.0)))
    rowscale = jnp.exp(jax.random.uniform(subkeys[4], lead_shape + (1,), jnp.float32, 0.0, math.log(10.0)))
    mixture = gaussian
    return (mixture * columns * rowscale / 21.5).astype(jnp.bfloat16)


def draw_lead_front(key, part):
    key = jax.random.fold_in(key, 11)
    return make_field(key, (SECTIONS, TOKENS))


def draw_mirror_front(key, part):
    key = jax.random.fold_in(key, 12)
    return make_field(key, (SECTIONS, TOKENS))


def draw_lead_grad(key, part):
    key = jax.random.fold_in(key, 13)
    return make_field(key, (SECTIONS, TOKENS))


def draw_mirror_grad(key, part):
    key = jax.random.fold_in(key, 14)
    return make_field(key, (SECTIONS, TOKENS))


def draw_lead_saved(key, part):
    key = jax.random.fold_in(key, 15)
    return make_field(key, (SECTIONS, TICKS, TOKENS))


def draw_mirror_saved(key, part):
    key = jax.random.fold_in(key, 16)
    return make_field(key, (SECTIONS, TICKS, TOKENS))


def level_of(own_key, dims, pieces, low, high):
    def one(position, blocks):
        steps = jax.random.uniform(jax.random.fold_in(jax.random.fold_in(own_key, 6), position), (blocks,), jnp.float32, low / len(pieces), high / len(pieces))
        return jnp.repeat(jnp.exp(steps), dims[position] // blocks).reshape((-1,) + (1,) * (len(dims) - position - 1))

    loudness = one(*pieces[0])
    for cut in pieces[1:]:
        loudness = loudness * one(*cut)
    return loudness


def centred(own_key, extent, scale, most, shards=(), dtype=jnp.bfloat16):
    factor_of = level_of(own_key, extent, shards, -0.22, 0.18) if shards else 1.0
    result = jax.random.normal(own_key, extent, jnp.float32) * scale * factor_of
    return jnp.minimum(jnp.maximum(result, -most), most).astype(dtype)


def setup_inputs(seed: int = 0) -> dict:
    seeds = jax.random.split(jax.random.key(seed), 11)
    return {
        "lead_front": draw_lead_front(jax.random.fold_in(seeds[10], 71), 0),
        "mirror_front": draw_mirror_front(jax.random.fold_in(seeds[10], 71), 0),
        "lead_grad": draw_lead_grad(jax.random.fold_in(seeds[10], 71), 0),
        "mirror_grad": draw_mirror_grad(jax.random.fold_in(seeds[10], 71), 0),
        "lead_saved": draw_lead_saved(jax.random.fold_in(seeds[10], 71), 0),
        "mirror_saved": draw_mirror_saved(jax.random.fold_in(seeds[10], 71), 0),
        "lead_down": centred(seeds[6], (SECTIONS, D, R), D ** -0.5, 0.109375, ((0, 64), (1, 4))),
        "lead_up": centred(seeds[7], (SECTIONS, R, D), R ** -0.5, 0.375, ((0, 64), (2, 4))),
        "mirror_down": centred(seeds[8], (SECTIONS, D, R), D ** -0.5, 0.109375, ((0, 64), (1, 4))),
        "mirror_up": centred(seeds[9], (SECTIONS, R, D), R ** -0.5, 0.375, ((0, 64), (2, 4))),
    }


EPS = 1e-06

def normalize(inputs):
    float_in = inputs.astype(jnp.float32)
    factor = lax.rsqrt(lax.optimization_barrier(jnp.mean(float_in * float_in, axis=-1, keepdims=True)) + EPS)
    return (float_in, factor)

def section_forward(inputs, w_down, w_up):
    float_in, factor = normalize(inputs)
    normed = (float_in * factor).astype(jnp.bfloat16)
    latent = jnp.einsum('snd,sdr->snr', normed.astype(jnp.float32), w_down)
    active = jax.nn.silu(latent).astype(jnp.bfloat16)
    branch = jnp.einsum('snr,srd->snd', active.astype(jnp.float32), w_up)
    return (float_in + branch).astype(jnp.bfloat16)

def section_backward(stored, incoming, w_down, w_up):
    float_in, factor = normalize(stored)
    scaled = float_in * factor
    normed = scaled.astype(jnp.bfloat16)
    latent = jnp.einsum('snd,sdr->snr', normed.astype(jnp.float32), w_down)
    active = jax.nn.silu(latent).astype(jnp.bfloat16)
    float_grad = incoming.astype(jnp.float32)
    d_active = jnp.einsum('snd,srd->snr', float_grad, w_up)
    squash = jax.nn.sigmoid(latent)
    d_latent = (d_active * squash * (1.0 + latent * (1.0 - squash))).astype(jnp.bfloat16)
    d_normed = jnp.einsum('snr,sdr->snd', d_latent.astype(jnp.float32), w_down)
    inner_mean = lax.optimization_barrier(jnp.mean(d_normed * scaled, axis=-1, keepdims=True))
    d_inputs = (float_grad + factor * (d_normed - scaled * inner_mean)).astype(jnp.bfloat16)
    grad_down = jnp.einsum('snd,snr->sdr', normed.astype(jnp.float32), d_latent.astype(jnp.float32))
    grad_up = jnp.einsum('snr,snd->srd', active.astype(jnp.float32), float_grad)
    return (d_inputs, grad_down, grad_up)

def shift_up(blocks):
    return jnp.concatenate([jnp.zeros_like(blocks[:1]), blocks[:-1]], axis=0)

def shift_down(blocks):
    return jnp.concatenate([blocks[1:], jnp.zeros_like(blocks[:1])], axis=0)

def reference(lead_front, mirror_front, lead_grad, mirror_grad, lead_saved, mirror_saved, lead_down, lead_up, mirror_down, mirror_up):
    weight_pairs = ((lead_down.astype(jnp.float32), lead_up.astype(jnp.float32)), (mirror_down.astype(jnp.float32), mirror_up.astype(jnp.float32)))
    stored = (lead_saved, mirror_saved)
    fronts = [lead_front, mirror_front]
    arriving = [lead_grad, mirror_grad]
    totals = [[jnp.zeros(lead_down.shape, jnp.float32), jnp.zeros(lead_up.shape, jnp.float32)], [jnp.zeros(mirror_down.shape, jnp.float32), jnp.zeros(mirror_up.shape, jnp.float32)]]
    for moment in range(TICKS):
        produced = []
        returned = []
        for member in range(2):
            w_down, w_up = weight_pairs[member]
            produced.append(section_forward(fronts[member], w_down, w_up))
            d_inputs, grad_down, grad_up = section_backward(stored[member][:, moment], arriving[member], w_down, w_up)
            returned.append(d_inputs)
            totals[member][0] = totals[member][0] + grad_down
            totals[member][1] = totals[member][1] + grad_up
        if moment + 1 < TICKS:
            fronts = [shift_up(produced[0]), shift_down(produced[1])]
            arriving = [shift_down(returned[0]), shift_up(returned[1])]
        else:
            fronts = produced
            arriving = returned
    return (fronts[0], fronts[1], arriving[0], arriving[1], totals[0][0].astype(jnp.bfloat16), totals[0][1].astype(jnp.bfloat16), totals[1][0].astype(jnp.bfloat16), totals[1][1].astype(jnp.bfloat16))
```

```python
import functools

import jax
import jax.numpy as jnp
from jax import lax
from jax.experimental import pallas as pl
from jax.experimental.pallas import tpu as pltpu
from jax.sharding import PartitionSpec as P

EPS = 1e-06
MESH = pl.DeviceIdType.MESH
BF16 = jnp.bfloat16
F32 = jnp.float32
NT = (((1,), (1,)), ((), ()))


def dot(a, b):
    return jnp.dot(a, b, preferred_element_type=F32)


def dot_nt(a, b):
    return lax.dot_general(a, b, NT, preferred_element_type=F32)


def kernel(
    lf, mf, lg, mg, ls, ms, ld, lu, md, mu,
    o_lf, o_mf, o_lb, o_mb, o_ld, o_lu, o_md, o_mu,
    wd, wu, sv, svt, sc, gb, xb, yb, bb, ob, dl, at, rsd, rsu, gsd, gsu,
    in_sem, out_sem, ag_s, ag_r, pp_s, pp_r, rs_s, rs_r,
):
    p, d = lax.axis_index("pipe"), lax.axis_index("dp")
    stages = lax.axis_size("pipe")
    _, _, rows, width = sv.shape
    shard = wd.shape[2]
    tile = min(256, shard)
    subs = shard // tile
    fronts, grads, saved = (lf, mf), (lg, mg), (ls, ms)
    downs, ups = (ld, md), (lu, mu)
    has_up, has_down = p < stages - 1, p > 0
    has_right, has_left = d < 3, d > 0
    is_end = (d == 0) | (d == 3)
    is_mid = (d == 1) | (d == 2)

    def local(src, dst, n):
        return pltpu.make_async_copy(src, dst, in_sem.at[n])

    loads = {}
    for m in range(2):
        loads["s", m] = local(saved[m].at[0], sv.at[m], m)
        loads["wd", m] = local(downs[m].at[0], wd.at[m, d], 2 + m)
        loads["wu", m] = local(ups[m].at[0], wu.at[m, d], 4 + m)
        loads["g", m] = local(grads[m].at[0], gb.at[m, pl.ds(0, rows)], 6 + m)
        loads["x", m] = local(fronts[m].at[0], xb.at[m, 0], 8 + m)
    for copy in loads.values():
        copy.start()

    barrier = pltpu.get_barrier_semaphore()
    around = (
        (has_up, (p + 1, d)),
        (has_down, (p - 1, d)),
        (has_right, (p, d + 1)),
        (has_left, (p, d - 1)),
    )
    for here, where in around:

        @pl.when(here)
        def _(where=where):
            pl.semaphore_signal(barrier, inc=1, device_id=where, device_id_type=MESH)

    pl.semaphore_wait(barrier, sum(here.astype(jnp.int32) for here, _ in around))

    def ag_copy(m, f, k, kind):
        index = jnp.clip(d - k if f == 0 else d + k, 0, 3)
        whole = (wd, wu)[kind]
        own = (downs, ups)[kind][m]
        return pltpu.make_async_remote_copy(
            src_ref=own.at[0] if k == 0 else whole.at[m, index],
            dst_ref=whole.at[m, index],
            send_sem=ag_s.at[f, m, kind, k],
            recv_sem=ag_r.at[f, m, kind, k],
            device_id=(p, d + 1 if f == 0 else d - 1),
            device_id_type=MESH,
        )

    def ag_sends(f, k):
        return has_right & (d >= k) if f == 0 else has_left & (d + k <= 3)

    def ag_send(m, f, k, here):
        @pl.when(here & ag_sends(f, k))
        def _():
            for kind in range(2):
                ag_copy(m, f, k, kind).start()

    def ag_arrived(m, f, k):
        index = jnp.clip(d - 1 - k if f == 0 else d + 1 + k, 0, 3)
        for kind in range(2):
            whole = (wd, wu)[kind]
            pltpu.make_async_remote_copy(
                src_ref=whole.at[m, index],
                dst_ref=whole.at[m, index],
                send_sem=ag_s.at[f, m, kind, k],
                recv_sem=ag_r.at[f, m, kind, k],
                device_id=(p, d + 1 if f == 0 else d - 1),
                device_id_type=MESH,
            ).wait_recv()

    def ag_forward(m, f, k):
        @pl.when(ag_sends(f, k))
        def _():
            ag_arrived(m, f, k - 1)
            for kind in range(2):
                ag_copy(m, f, k, kind).start()

    def ag_ends(m):
        for f, last in ((0, 3), (1, 0)):

            @pl.when(d == last)
            def _(f=f):
                for k in range(3):
                    ag_arrived(m, f, k)

    def columns(o, s):
        return pl.ds(pl.multiple_of(o * shard + s * tile, tile), tile)

    def block(o):
        return pl.ds(pl.multiple_of(o * shard, shard), shard)

    def scale_of(ref):
        def add(o, total):
            for s in range(subs):
                x = ref[:, columns(o, s)].astype(F32)
                total = total + x * x
            return total

        total = lax.fori_loop(0, 4, add, jnp.zeros((rows, tile), F32))
        return lax.rsqrt(jnp.sum(total, axis=1, keepdims=True) / width + EPS)

    def prepare(m, t):
        ref = sv.at[m, t]
        factor = scale_of(ref)
        sc[m, t] = jnp.broadcast_to(factor, (rows, 128))

        def step(o, carry):
            for s in range(subs):
                here = columns(o, s)
                normed = ref[:, here].astype(F32) * factor
                ref[:, here] = normed.astype(BF16)
                svt[m, here, t * rows : (t + 1) * rows] = normed.T.astype(BF16)
            return carry

        lax.fori_loop(0, 4, step, 0)

    def forward(m, t, out):
        ref = xb.at[m, t]
        factor = scale_of(ref)

        def down(o, total):
            for s in range(subs):
                normed = (ref[:, columns(o, s)].astype(F32) * factor).astype(BF16)
                total = total + dot(normed, wd[m, o, s * tile : (s + 1) * tile, :])
            return total

        latent = lax.fori_loop(0, 4, down, jnp.zeros((rows, wd.shape[3]), F32))
        active = (latent * jax.nn.sigmoid(latent)).astype(BF16)

        def up(o, carry):
            for s in range(subs):
                here = columns(o, s)
                branch = dot(active, wu[m, o, :, s * tile : (s + 1) * tile])
                out[:, here] = (ref[:, here].astype(F32) + branch).astype(BF16)
            return carry

        lax.fori_loop(0, 4, up, 0)

    def backward(m, t, out):
        ref = sv.at[m, t]
        incoming = gb.at[m, pl.ds(t * rows, rows)]
        zero = jnp.zeros((rows, wd.shape[3]), F32)

        def down(o, total):
            latent, d_active = total
            latent = latent + dot(ref[:, block(o)], wd[m, o])
            d_active = d_active + dot_nt(incoming[:, block(o)], wu[m, o])
            return latent, d_active

        latent, d_active = lax.fori_loop(0, 4, down, (zero, zero))
        squash = jax.nn.sigmoid(latent)
        active = latent * squash
        d_latent = (d_active * squash * (1.0 + latent * (1.0 - squash))).astype(BF16)
        dl[m, t * rows : (t + 1) * rows, :] = d_latent
        at[m, :, t * rows : (t + 1) * rows] = active.T.astype(BF16)
        inner = jnp.sum(d_latent.astype(F32) * latent, axis=1, keepdims=True) / width
        factor = sc[m, t][:, 0:1]

        def up(o, carry):
            for s in range(subs):
                here = columns(o, s)
                d_normed = dot_nt(d_latent, wd[m, o, s * tile : (s + 1) * tile, :])
                scaled = ref[:, here].astype(F32)
                out[:, here] = (
                    incoming[:, here].astype(F32) + factor * (d_normed - scaled * inner)
                ).astype(BF16)
            return carry

        lax.fori_loop(0, 4, up, 0)

    def pipe_copy(n):
        m = n % 2
        src = yb.at[m] if n < 2 else bb.at[m]
        dst = xb.at[m, 1] if n < 2 else gb.at[m, pl.ds(rows, rows)]
        return pltpu.make_async_remote_copy(
            src_ref=src,
            dst_ref=dst,
            send_sem=pp_s.at[n],
            recv_sem=pp_r.at[n],
            device_id=(p + 1 if n in (0, 3) else p - 1, d),
            device_id_type=MESH,
        )

    def pipe_ends(n):
        return (has_up, has_down) if n in (0, 3) else (has_down, has_up)

    def pipe_send(n):
        @pl.when(pipe_ends(n)[0])
        def _():
            pipe_copy(n).start()

    def pipe_wait(n):
        arrives = pipe_ends(n)[1]

        @pl.when(arrives)
        def _():
            pipe_copy(n).wait_recv()

        @pl.when(jnp.logical_not(arrives))
        def _():
            m = n % 2
            if n < 2:
                xb[m, 1] = jnp.zeros((rows, width), BF16)
            else:
                gb[m, rows : 2 * rows, :] = jnp.zeros((rows, width), BF16)

    def rs_copy(m, f, j, kind, target):
        held = (rsd, rsu)[kind]
        return pltpu.make_async_remote_copy(
            src_ref=held.at[f, m, j],
            dst_ref=held.at[f, m, j],
            send_sem=rs_s.at[f, m, j, kind],
            recv_sem=rs_r.at[f, m, j, kind],
            device_id=(p, target),
            device_id_type=MESH,
        )

    def piece(m, o, kind, out, arrived=()):
        for s in range(subs):
            if kind == 0:
                here = (slice(s * tile, (s + 1) * tile), slice(None))
                part = dot(svt[m, columns(o, s), :], dl[m])
            else:
                here = (slice(None), slice(s * tile, (s + 1) * tile))
                part = dot(at[m], gb[m, :, columns(o, s)])
            for ref in arrived:
                part = part + ref[here].astype(F32)
            out[here] = part.astype(BF16)

    flow = jnp.where(d == 0, 0, 1)

    def rs_ends(m, j):
        @pl.when(is_end)
        def _():
            owner = jnp.where(d == 0, 3 - j, j)
            for kind in range(2):
                piece(m, owner, kind, (rsd, rsu)[kind].at[flow, m, j])
                rs_copy(m, flow, j, kind, jnp.where(d == 0, 1, 2)).start()

    def rs_passes(f, j):
        return is_mid & ((d < 3 - j) if f == 0 else (d > j))

    def rs_mids(m):
        for j in range(2):
            for kind in range(2):
                for f in range(2):

                    @pl.when(rs_passes(f, j))
                    def _(j=j, kind=kind, f=f):
                        copy = rs_copy(m, f, j, kind, d + 1 if f == 0 else d - 1)
                        copy.wait_recv()
                        held = (rsd, rsu)[kind].at[f, m, j]
                        piece(m, 3 - j if f == 0 else j, kind, held, (held,))
                        copy.start()

    def rs_finish(m):
        for kind in range(2):
            held, out = (rsd, rsu)[kind], (gsd, gsu)[kind].at[m]

            @pl.when(is_end)
            def _():
                rs_copy(m, 1 - flow, 0, kind, jnp.where(d == 0, 1, 2)).wait_recv()
                piece(m, d, kind, out, (held.at[1 - flow, m, 0],))

            @pl.when(is_mid)
            def _():
                rs_copy(m, 0, 3 - d, kind, d + 1).wait_recv()
                rs_copy(m, 1, d, kind, d - 1).wait_recv()
                piece(m, d, kind, out, (held.at[0, m, 3 - d], held.at[1, m, d]))

    results = (
        (ob.at[0], o_lf), (ob.at[1], o_mf), (ob.at[2], o_lb), (ob.at[3], o_mb),
        (gsd.at[0], o_ld), (gsu.at[0], o_lu), (gsd.at[1], o_md), (gsu.at[1], o_mu),
    )

    def result(n):
        return pltpu.make_async_copy(results[n][0], results[n][1].at[0], out_sem.at[n])

    everyone = d >= 0
    for f in range(2):
        ag_send(0, f, 0, everyone)
    for m in range(2):
        loads["s", m].wait()
        for t in range(2):
            prepare(m, t)
    for key in ("wd", "wu", "g", "x"):
        for m in range(2):
            loads[key, m].wait()
    for f in range(2):
        ag_forward(0, f, 1)
        ag_send(1, f, 0, d == (0, 3)[f])
    for f in range(2):
        ag_forward(0, f, 2)
        ag_send(1, f, 0, d == (1, 2)[f])
    ag_ends(0)

    backward(0, 0, bb.at[0])
    pipe_send(2)
    for f in range(2):
        ag_send(1, f, 0, d == (2, 1)[f])
    forward(0, 0, yb.at[0])
    pipe_send(0)

    for f in range(2):
        ag_forward(1, f, 1)
    for f in range(2):
        ag_forward(1, f, 2)

    pipe_wait(2)
    backward(0, 1, ob.at[2])
    result(2).start()
    rs_ends(0, 0)
    rs_ends(0, 1)
    pipe_wait(0)
    forward(0, 1, ob.at[0])
    result(0).start()

    ag_ends(1)
    backward(1, 0, bb.at[1])
    pipe_send(3)
    rs_ends(0, 2)
    forward(1, 0, yb.at[1])
    pipe_send(1)

    pipe_wait(3)
    backward(1, 1, ob.at[3])
    result(3).start()
    rs_ends(1, 0)
    rs_ends(1, 1)
    rs_ends(1, 2)
    rs_mids(0)
    pipe_wait(1)
    forward(1, 1, ob.at[1])
    result(1).start()
    rs_finish(0)
    result(4).start()
    result(5).start()
    rs_mids(1)
    rs_finish(1)
    result(6).start()
    result(7).start()

    for m in range(2):
        for f in range(2):
            for k in range(3):

                @pl.when(ag_sends(f, k))
                def _(m=m, f=f, k=k):
                    for kind in range(2):
                        ag_copy(m, f, k, kind).wait_send()

    for n in range(4):

        @pl.when(pipe_ends(n)[0])
        def _(n=n):
            pipe_copy(n).wait_send()

    for m in range(2):

        @pl.when(is_end)
        def _(m=m):
            for j in range(3):
                for kind in range(2):
                    rs_copy(m, flow, j, kind, jnp.where(d == 0, 1, 2)).wait_send()

        for j in range(2):
            for f in range(2):

                @pl.when(rs_passes(f, j))
                def _(m=m, j=j, f=f):
                    for kind in range(2):
                        rs_copy(m, f, j, kind, d + 1 if f == 0 else d - 1).wait_send()

    for n in range(8):
        result(n).wait()


def body(*arrays):
    lf, ls, ld, lu = arrays[0], arrays[4], arrays[6], arrays[7]
    _, ticks, rows, width = ls.shape
    _, shard, latents = ld.shape
    outs = [jax.ShapeDtypeStruct(lf.shape, BF16)] * 4 + [
        jax.ShapeDtypeStruct(ld.shape, BF16),
        jax.ShapeDtypeStruct(lu.shape, BF16),
    ] * 2
    vmem = pltpu.VMEM
    dma = pltpu.SemaphoreType.DMA
    return pl.pallas_call(
        kernel,
        out_shape=outs,
        in_specs=[pl.BlockSpec(memory_space=pl.ANY)] * 10,
        out_specs=[pl.BlockSpec(memory_space=pl.ANY)] * 8,
        scratch_shapes=[
            vmem((2, 4, shard, latents), BF16),
            vmem((2, 4, latents, shard), BF16),
            vmem((2, ticks, rows, width), BF16),
            vmem((2, width, ticks * rows), BF16),
            vmem((2, ticks, rows, 128), F32),
            vmem((2, ticks * rows, width), BF16),
            vmem((2, ticks, rows, width), BF16),
            vmem((2, rows, width), BF16),
            vmem((2, rows, width), BF16),
            vmem((4, rows, width), BF16),
            vmem((2, ticks * rows, latents), BF16),
            vmem((2, latents, ticks * rows), BF16),
            vmem((2, 2, 3, shard, latents), BF16),
            vmem((2, 2, 3, latents, shard), BF16),
            vmem((2, shard, latents), BF16),
            vmem((2, latents, shard), BF16),
            dma((10,)),
            dma((8,)),
            dma((2, 2, 2, 3)),
            dma((2, 2, 2, 3)),
            dma((4,)),
            dma((4,)),
            dma((2, 2, 3, 2)),
            dma((2, 2, 3, 2)),
        ],
        compiler_params=pltpu.CompilerParams(
            collective_id=0, has_side_effects=True, vmem_limit_bytes=52 * 2**20
        ),
        name="relay_window",
    )(*arrays)


def solution(mesh):
    front = P("pipe", "dp", None)
    up = P("pipe", None, "dp")
    placed = (front,) * 4 + (P("pipe", None, "dp", None),) * 2 + (front, up, front, up)
    return jax.shard_map(
        body,
        mesh=mesh,
        in_specs=placed,
        out_specs=(front,) * 4 + (front, up, front, up),
        check_vma=False,
    )
```

```python
import functools

import jax
import jax.numpy as jnp
from jax import lax
from jax.experimental import pallas as pl
from jax.experimental.pallas import tpu as pltpu
from jax.sharding import PartitionSpec as P

EPS = 1e-06
MESH = pl.DeviceIdType.MESH
BF16 = jnp.bfloat16
F32 = jnp.float32
NT = (((1,), (1,)), ((), ()))


def dot(a, b):
    return jnp.dot(a, b, preferred_element_type=F32)


def dot_nt(a, b):
    return lax.dot_general(a, b, NT, preferred_element_type=F32)


def kernel(
    lf, mf, lg, mg, ls, ms, ld, lu, md, mu,
    o_lf, o_mf, o_lb, o_mb, o_ld, o_lu, o_md, o_mu,
    wd, wu, sv, svt, sc, gb, xb, yb, bb, ob, dl, at, rsd, rsu, gsd, gsu,
    in_sem, out_sem, ag_s, ag_r, pp_s, pp_r, rs_s, rs_r,
):
    p, d = lax.axis_index("pipe"), lax.axis_index("dp")
    stages = lax.axis_size("pipe")
    _, _, rows, width = sv.shape
    shard = wd.shape[2]
    tile = min(256, shard)
    subs = shard // tile
    fronts, grads, saved = (lf, mf), (lg, mg), (ls, ms)
    downs, ups = (ld, md), (lu, mu)
    has_up, has_down = p < stages - 1, p > 0
    has_right, has_left = d < 3, d > 0
    is_end = (d == 0) | (d == 3)
    is_mid = (d == 1) | (d == 2)

    def local(src, dst, n):
        return pltpu.make_async_copy(src, dst, in_sem.at[n])

    loads = {}
    for m in range(2):
        loads["s", m] = local(saved[m].at[0], sv.at[m], m)
        loads["wd", m] = local(downs[m].at[0], wd.at[m, d], 2 + m)
        loads["wu", m] = local(ups[m].at[0], wu.at[m, d], 4 + m)
        loads["g", m] = local(grads[m].at[0], gb.at[m, pl.ds(0, rows)], 6 + m)
        loads["x", m] = local(fronts[m].at[0], xb.at[m, 0], 8 + m)
    for copy in loads.values():
        copy.start()

    barrier = pltpu.get_barrier_semaphore()
    around = (
        (has_up, (p + 1, d)),
        (has_down, (p - 1, d)),
        (has_right, (p, d + 1)),
        (has_left, (p, d - 1)),
    )
    for here, where in around:

        @pl.when(here)
        def _(where=where):
            pl.semaphore_signal(barrier, inc=1, device_id=where, device_id_type=MESH)

    pl.semaphore_wait(barrier, sum(here.astype(jnp.int32) for here, _ in around))

    out_to, out_flow = jnp.where(d == 0, 1, 2), jnp.where(d == 0, 0, 1)
    cross_to, cross_flow = 3 - d, jnp.clip(d - 1, 0, 1)
    end_to, end_flow = jnp.where(d == 1, 0, 3), jnp.clip(2 - d, 0, 1)

    def ag_copy(m, kind, flow, step, shard_of, target, own=False):
        whole = (wd, wu)[kind]
        return pltpu.make_async_remote_copy(
            src_ref=(downs, ups)[kind][m].at[0] if own else whole.at[m, shard_of],
            dst_ref=whole.at[m, shard_of],
            send_sem=ag_s.at[flow, m, kind, step],
            recv_sem=ag_r.at[flow, m, kind, step],
            device_id=(p, target),
            device_id_type=MESH,
        )

    def own_from_end(m, kind):
        @pl.when(is_end)
        def _():
            ag_copy(m, kind, out_flow, 0, d, out_to, True).start()

    def own_across(m, kind):
        @pl.when(is_mid)
        def _():
            ag_copy(m, kind, cross_flow, 0, d, cross_to, True).start()

    def own_to_end(m, kind):
        @pl.when(is_mid)
        def _():
            ag_copy(m, kind, end_flow, 0, d, end_to, True).start()

    def pass_across(m, kind):
        @pl.when(is_mid)
        def _():
            ag_copy(m, kind, cross_flow, 0, end_to, cross_to).wait_recv()
            ag_copy(m, kind, cross_flow, 1, end_to, cross_to).start()

    def pass_to_end(m, kind, step):
        shard_of = cross_to if step == 1 else 3 - end_to

        @pl.when(is_mid)
        def _():
            ag_copy(m, kind, end_flow, step - 1, shard_of, end_to).wait_recv()
            ag_copy(m, kind, end_flow, step, shard_of, end_to).start()

    def end_gathers(m):
        @pl.when(is_end)
        def _():
            for step in range(3):
                shard_of = jnp.where(d == 0, 1 + step, 2 - step)
                for kind in range(2):
                    ag_copy(m, kind, 1 - out_flow, step, shard_of, out_to).wait_recv()

    def columns(o, s):
        return pl.ds(pl.multiple_of(o * shard + s * tile, tile), tile)

    def block(o):
        return pl.ds(pl.multiple_of(o * shard, shard), shard)

    def scale_of(ref):
        def add(o, total):
            for s in range(subs):
                x = ref[:, columns(o, s)].astype(F32)
                total = total + x * x
            return total

        total = lax.fori_loop(0, 4, add, jnp.zeros((rows, tile), F32))
        return lax.rsqrt(jnp.sum(total, axis=1, keepdims=True) / width + EPS)

    def prepare(m, t):
        ref = sv.at[m, t]
        factor = scale_of(ref)
        sc[m, t] = jnp.broadcast_to(factor, (rows, 128))

        def step(o, carry):
            for s in range(subs):
                here = columns(o, s)
                normed = ref[:, here].astype(F32) * factor
                ref[:, here] = normed.astype(BF16)
                svt[m, here, t * rows : (t + 1) * rows] = normed.T.astype(BF16)
            return carry

        lax.fori_loop(0, 4, step, 0)

    def forward(m, t, out):
        ref = xb.at[m, t]
        factor = scale_of(ref)

        def down(o, total):
            for s in range(subs):
                normed = (ref[:, columns(o, s)].astype(F32) * factor).astype(BF16)
                total = total + dot(normed, wd[m, o, s * tile : (s + 1) * tile, :])
            return total

        latent = lax.fori_loop(0, 4, down, jnp.zeros((rows, wd.shape[3]), F32))
        active = (latent * jax.nn.sigmoid(latent)).astype(BF16)

        def up(o, carry):
            for s in range(subs):
                here = columns(o, s)
                branch = dot(active, wu[m, o, :, s * tile : (s + 1) * tile])
                out[:, here] = (ref[:, here].astype(F32) + branch).astype(BF16)
            return carry

        lax.fori_loop(0, 4, up, 0)

    def backward(m, t, out):
        ref = sv.at[m, t]
        incoming = gb.at[m, pl.ds(t * rows, rows)]
        zero = jnp.zeros((rows, wd.shape[3]), F32)

        def down(o, total):
            latent, d_active = total
            latent = latent + dot(ref[:, block(o)], wd[m, o])
            d_active = d_active + dot_nt(incoming[:, block(o)], wu[m, o])
            return latent, d_active

        latent, d_active = lax.fori_loop(0, 4, down, (zero, zero))
        squash = jax.nn.sigmoid(latent)
        active = latent * squash
        d_latent = (d_active * squash * (1.0 + latent * (1.0 - squash))).astype(BF16)
        dl[m, t * rows : (t + 1) * rows, :] = d_latent
        at[m, :, t * rows : (t + 1) * rows] = active.T.astype(BF16)
        inner = jnp.sum(d_latent.astype(F32) * latent, axis=1, keepdims=True) / width
        factor = sc[m, t][:, 0:1]

        def up(o, carry):
            for s in range(subs):
                here = columns(o, s)
                d_normed = dot_nt(d_latent, wd[m, o, s * tile : (s + 1) * tile, :])
                scaled = ref[:, here].astype(F32)
                out[:, here] = (
                    incoming[:, here].astype(F32) + factor * (d_normed - scaled * inner)
                ).astype(BF16)
            return carry

        lax.fori_loop(0, 4, up, 0)

    def pipe_copy(n):
        m = n % 2
        src = yb.at[m] if n < 2 else bb.at[m]
        dst = xb.at[m, 1] if n < 2 else gb.at[m, pl.ds(rows, rows)]
        return pltpu.make_async_remote_copy(
            src_ref=src,
            dst_ref=dst,
            send_sem=pp_s.at[n],
            recv_sem=pp_r.at[n],
            device_id=(p + 1 if n in (0, 3) else p - 1, d),
            device_id_type=MESH,
        )

    def pipe_ends(n):
        return (has_up, has_down) if n in (0, 3) else (has_down, has_up)

    def pipe_send(n, far):
        first = lax.rem(p, 2) == 0
        near = first if n in (0, 3) else jnp.logical_not(first)

        @pl.when(pipe_ends(n)[0] & (jnp.logical_not(near) if far else near))
        def _():
            pipe_copy(n).start()

    def pipe_wait(n):
        arrives = pipe_ends(n)[1]

        @pl.when(arrives)
        def _():
            pipe_copy(n).wait_recv()

        @pl.when(jnp.logical_not(arrives))
        def _():
            m = n % 2
            if n < 2:
                xb[m, 1] = jnp.zeros((rows, width), BF16)
            else:
                gb[m, rows : 2 * rows, :] = jnp.zeros((rows, width), BF16)

    def rs_copy(m, f, j, kind, target):
        held = (rsd, rsu)[kind]
        return pltpu.make_async_remote_copy(
            src_ref=held.at[f, m, j],
            dst_ref=held.at[f, m, j],
            send_sem=rs_s.at[f, m, j, kind],
            recv_sem=rs_r.at[f, m, j, kind],
            device_id=(p, target),
            device_id_type=MESH,
        )

    def piece(m, o, kind, out, arrived=()):
        for s in range(subs):
            if kind == 0:
                here = (slice(s * tile, (s + 1) * tile), slice(None))
                part = dot(svt[m, columns(o, s), :], dl[m])
            else:
                here = (slice(None), slice(s * tile, (s + 1) * tile))
                part = dot(at[m], gb[m, :, columns(o, s)])
            for ref in arrived:
                part = part + ref[here].astype(F32)
            out[here] = part.astype(BF16)

    def grad_from_end(m, j, kind):
        @pl.when(is_end)
        def _():
            owner = jnp.where(d == 0, 3 - j, j)
            piece(m, owner, kind, (rsd, rsu)[kind].at[out_flow, m, j])
            rs_copy(m, out_flow, j, kind, out_to).start()

    def grad_across(m, j, kind):
        @pl.when(is_mid)
        def _():
            owner = jnp.where(d == 1, 3 - j, j)
            copy = rs_copy(m, cross_flow, j, kind, cross_to)
            copy.wait_recv()
            held = (rsd, rsu)[kind].at[cross_flow, m, j]
            piece(m, owner, kind, held, (held,))
            copy.start()

    def grad_to_end(m, kind):
        @pl.when(is_mid)
        def _():
            copy = rs_copy(m, end_flow, 0, kind, end_to)
            copy.wait_recv()
            held = (rsd, rsu)[kind].at[end_flow, m, 0]
            piece(m, end_to, kind, held, (held,))
            copy.start()

    def grad_finish(m):
        for kind in range(2):
            held, out = (rsd, rsu)[kind], (gsd, gsu)[kind].at[m]

            @pl.when(is_end)
            def _():
                rs_copy(m, 1 - out_flow, 0, kind, out_to).wait_recv()
                piece(m, d, kind, out, (held.at[1 - out_flow, m, 0],))

            @pl.when(is_mid)
            def _():
                rs_copy(m, cross_flow, 2, kind, cross_to).wait_recv()
                rs_copy(m, end_flow, 1, kind, end_to).wait_recv()
                piece(m, d, kind, out, (held.at[cross_flow, m, 2], held.at[end_flow, m, 1]))

            result(4 + 2 * m + kind).start()

    results = (
        (ob.at[0], o_lf), (ob.at[1], o_mf), (ob.at[2], o_lb), (ob.at[3], o_mb),
        (gsd.at[0], o_ld), (gsu.at[0], o_lu), (gsd.at[1], o_md), (gsu.at[1], o_mu),
    )

    def result(n):
        return pltpu.make_async_copy(results[n][0], results[n][1].at[0], out_sem.at[n])

    own_to_end(0, 1)
    own_from_end(0, 1)
    own_across(0, 1)
    own_to_end(0, 0)
    own_across(0, 0)
    pass_to_end(0, 1, 1)
    pass_across(0, 1)
    own_from_end(0, 0)
    loads["s", 0].wait()
    prepare(0, 0)
    prepare(0, 1)
    loads["s", 1].wait()
    prepare(1, 0)
    prepare(1, 1)
    pass_across(0, 0)
    own_across(1, 0)
    pass_to_end(0, 0, 1)
    pass_to_end(0, 1, 2)
    own_from_end(1, 0)
    pass_to_end(0, 0, 2)
    own_from_end(1, 1)
    loads["wd", 0].wait()
    loads["wu", 0].wait()
    loads["g", 0].wait()
    end_gathers(0)
    backward(0, 0, bb.at[0])
    pipe_send(2, True)
    pipe_send(2, False)
    pipe_wait(2)
    backward(0, 1, ob.at[2])
    result(2).start()
    grad_from_end(0, 0, 1)
    grad_from_end(0, 1, 1)
    grad_from_end(0, 1, 0)
    pass_across(1, 1)
    loads["x", 0].wait()
    forward(0, 0, yb.at[0])
    pass_across(1, 0)
    pass_to_end(1, 0, 1)
    pass_to_end(1, 0, 2)
    own_to_end(1, 1)
    grad_across(0, 0, 1)
    own_across(1, 1)
    grad_from_end(0, 0, 0)
    grad_across(0, 1, 0)
    grad_from_end(0, 2, 1)
    grad_from_end(0, 2, 0)
    pass_to_end(1, 1, 1)
    pass_to_end(1, 1, 2)
    grad_across(0, 1, 1)
    own_to_end(1, 0)
    grad_across(0, 0, 0)
    loads["wd", 1].wait()
    loads["wu", 1].wait()
    loads["g", 1].wait()
    end_gathers(1)
    backward(1, 0, bb.at[1])
    pipe_send(3, True)
    pipe_send(3, False)
    loads["x", 1].wait()
    forward(1, 0, yb.at[1])
    pipe_send(0, True)
    pipe_wait(3)
    backward(1, 1, ob.at[3])
    result(3).start()
    grad_across(1, 0, 1)
    grad_to_end(0, 1)
    grad_to_end(1, 1)
    grad_across(1, 0, 0)
    grad_from_end(1, 0, 1)
    grad_to_end(0, 0)
    grad_to_end(1, 0)
    pipe_send(0, False)
    grad_from_end(1, 0, 0)
    grad_from_end(1, 1, 1)
    grad_across(1, 1, 0)
    pipe_send(1, False)
    grad_from_end(1, 1, 0)
    grad_across(1, 1, 1)
    pipe_send(1, True)
    grad_from_end(1, 2, 0)
    grad_from_end(1, 2, 1)
    grad_finish(0)
    pipe_wait(0)
    forward(0, 1, ob.at[0])
    result(0).start()
    pipe_wait(1)
    forward(1, 1, ob.at[1])
    result(1).start()
    grad_finish(1)

    for m in range(2):
        for kind in range(2):

            @pl.when(is_end)
            def _(m=m, kind=kind):
                ag_copy(m, kind, out_flow, 0, d, out_to, True).wait_send()
                for j in range(3):
                    rs_copy(m, out_flow, j, kind, out_to).wait_send()

            @pl.when(is_mid)
            def _(m=m, kind=kind):
                for step in range(2):
                    ag_copy(m, kind, cross_flow, step, d, cross_to).wait_send()
                    rs_copy(m, cross_flow, step, kind, cross_to).wait_send()
                for step in range(3):
                    ag_copy(m, kind, end_flow, step, d, end_to).wait_send()
                rs_copy(m, end_flow, 0, kind, end_to).wait_send()

    for n in range(4):

        @pl.when(pipe_ends(n)[0])
        def _(n=n):
            pipe_copy(n).wait_send()

    for n in range(8):
        result(n).wait()


def body(*arrays):
    lf, ls, ld, lu = arrays[0], arrays[4], arrays[6], arrays[7]
    _, ticks, rows, width = ls.shape
    _, shard, latents = ld.shape
    outs = [jax.ShapeDtypeStruct(lf.shape, BF16)] * 4 + [
        jax.ShapeDtypeStruct(ld.shape, BF16),
        jax.ShapeDtypeStruct(lu.shape, BF16),
    ] * 2
    vmem = pltpu.VMEM
    dma = pltpu.SemaphoreType.DMA
    return pl.pallas_call(
        kernel,
        out_shape=outs,
        in_specs=[pl.BlockSpec(memory_space=pl.ANY)] * 10,
        out_specs=[pl.BlockSpec(memory_space=pl.ANY)] * 8,
        scratch_shapes=[
            vmem((2, 4, shard, latents), BF16),
            vmem((2, 4, latents, shard), BF16),
            vmem((2, ticks, rows, width), BF16),
            vmem((2, width, ticks * rows), BF16),
            vmem((2, ticks, rows, 128), F32),
            vmem((2, ticks * rows, width), BF16),
            vmem((2, ticks, rows, width), BF16),
            vmem((2, rows, width), BF16),
            vmem((2, rows, width), BF16),
            vmem((4, rows, width), BF16),
            vmem((2, ticks * rows, latents), BF16),
            vmem((2, latents, ticks * rows), BF16),
            vmem((2, 2, 3, shard, latents), BF16),
            vmem((2, 2, 3, latents, shard), BF16),
            vmem((2, shard, latents), BF16),
            vmem((2, latents, shard), BF16),
            dma((10,)),
            dma((8,)),
            dma((2, 2, 2, 3)),
            dma((2, 2, 2, 3)),
            dma((4,)),
            dma((4,)),
            dma((2, 2, 3, 2)),
            dma((2, 2, 3, 2)),
        ],
        compiler_params=pltpu.CompilerParams(
            collective_id=0, has_side_effects=True, vmem_limit_bytes=52 * 2**20
        ),
        name="relay_window",
    )(*arrays)


def solution(mesh):
    front = P("pipe", "dp", None)
    up = P("pipe", None, "dp")
    placed = (front,) * 4 + (P("pipe", None, "dp", None),) * 2 + (front, up, front, up)
    return jax.shard_map(
        body,
        mesh=mesh,
        in_specs=placed,
        out_specs=(front,) * 4 + (front, up, front, up),
        check_vma=False,
    )
```

```python
import functools

import jax
import jax.numpy as jnp
from jax import lax
from jax.experimental import pallas as pl
from jax.experimental.pallas import tpu as pltpu
from jax.sharding import PartitionSpec as P

EPS = 1e-06
MESH = pl.DeviceIdType.MESH
BF16 = jnp.bfloat16
F32 = jnp.float32
NT = (((1,), (1,)), ((), ()))


def dot(a, b):
    return jnp.dot(a, b, preferred_element_type=F32)


def dot_nt(a, b):
    return lax.dot_general(a, b, NT, preferred_element_type=F32)


def kernel(
    lf, mf, lg, mg, ls, ms, ld, lu, md, mu,
    o_lf, o_mf, o_lb, o_mb, o_ld, o_lu, o_md, o_mu,
    wd, wu, sv, svt, sc, gb, xb, yb, bb, ob, dl, at, rsd, rsu, gsd, gsu, far_n, far_dl, far_g, far_at,
    in_sem, out_sem, ag_s, ag_r, pp_s, pp_r, rs_s, rs_r, op_s, op_r, lt_s, lt_r,
):
    p, d = lax.axis_index("pipe"), lax.axis_index("dp")
    stages = lax.axis_size("pipe")
    _, _, rows, width = sv.shape
    shard = wd.shape[2]
    tile = min(256, shard)
    subs = shard // tile
    fronts, grads, saved = (lf, mf), (lg, mg), (ls, ms)
    downs, ups = (ld, md), (lu, mu)
    has_up, has_down = p < stages - 1, p > 0
    has_right, has_left = d < 3, d > 0
    is_end = (d == 0) | (d == 3)
    is_mid = (d == 1) | (d == 2)
    by_operands = ((), (0,))

    def local(src, dst, n):
        return pltpu.make_async_copy(src, dst, in_sem.at[n])

    loads = {}
    for m in range(2):
        loads["s", m] = local(saved[m].at[0], sv.at[m], m)
        loads["wd", m] = local(downs[m].at[0], wd.at[m, d], 2 + m)
        loads["wu", m] = local(ups[m].at[0], wu.at[m, d], 4 + m)
        loads["g", m] = local(grads[m].at[0], gb.at[m, pl.ds(0, rows)], 6 + m)
        loads["x", m] = local(fronts[m].at[0], xb.at[m, 0], 8 + m)
    for copy in loads.values():
        copy.start()

    barrier = pltpu.get_barrier_semaphore()
    around = (
        (has_up, (p + 1, d)),
        (has_down, (p - 1, d)),
        (has_right, (p, d + 1)),
        (has_left, (p, d - 1)),
    )
    for here, where in around:

        @pl.when(here)
        def _(where=where):
            pl.semaphore_signal(barrier, inc=1, device_id=where, device_id_type=MESH)

    pl.semaphore_wait(barrier, sum(here.astype(jnp.int32) for here, _ in around))

    out_to, out_flow = jnp.where(d == 0, 1, 2), jnp.where(d == 0, 0, 1)
    cross_to, cross_flow = 3 - d, jnp.clip(d - 1, 0, 1)
    end_to, end_flow = jnp.where(d == 1, 0, 3), jnp.clip(2 - d, 0, 1)

    def ag_copy(m, kind, flow, step, shard_of, target, own=False):
        whole = (wd, wu)[kind]
        return pltpu.make_async_remote_copy(
            src_ref=(downs, ups)[kind][m].at[0] if own else whole.at[m, shard_of],
            dst_ref=whole.at[m, shard_of],
            send_sem=ag_s.at[flow, m, kind, step],
            recv_sem=ag_r.at[flow, m, kind, step],
            device_id=(p, target),
            device_id_type=MESH,
        )

    def own_from_end(m, kind):
        @pl.when(is_end)
        def _():
            ag_copy(m, kind, out_flow, 0, d, out_to, True).start()

    def own_across(m, kind):
        @pl.when(is_mid)
        def _():
            ag_copy(m, kind, cross_flow, 0, d, cross_to, True).start()

    def own_to_end(m, kind):
        @pl.when(is_mid)
        def _():
            ag_copy(m, kind, end_flow, 0, d, end_to, True).start()

    def pass_across(m, kind):
        @pl.when(is_mid)
        def _():
            ag_copy(m, kind, cross_flow, 0, end_to, cross_to).wait_recv()
            ag_copy(m, kind, cross_flow, 1, end_to, cross_to).start()

    def pass_to_end(m, kind, step):
        shard_of = cross_to if step == 1 else 3 - end_to

        @pl.when(is_mid)
        def _():
            ag_copy(m, kind, end_flow, step - 1, shard_of, end_to).wait_recv()
            ag_copy(m, kind, end_flow, step, shard_of, end_to).start()

    def end_gathers(m):
        @pl.when(is_end)
        def _():
            for step in range(3):
                shard_of = jnp.where(d == 0, 1 + step, 2 - step)
                for kind in range(2):
                    ag_copy(m, kind, 1 - out_flow, step, shard_of, out_to).wait_recv()

    def columns(o, s):
        return pl.ds(pl.multiple_of(o * shard + s * tile, tile), tile)

    def block(o):
        return pl.ds(pl.multiple_of(o * shard, shard), shard)

    def scale_of(ref):
        def add(o, total):
            for s in range(subs):
                x = ref[:, columns(o, s)].astype(F32)
                total = total + x * x
            return total

        total = lax.fori_loop(0, 4, add, jnp.zeros((rows, tile), F32))
        return lax.rsqrt(jnp.sum(total, axis=1, keepdims=True) / width + EPS)

    def prepare(m, t):
        ref = sv.at[m, t]
        factor = scale_of(ref)
        sc[m, t] = jnp.broadcast_to(factor, (rows, 128))

        def step(o, carry):
            for s in range(subs):
                here = columns(o, s)
                normed = ref[:, here].astype(F32) * factor
                ref[:, here] = normed.astype(BF16)
                svt[m, here, t * rows : (t + 1) * rows] = normed.T.astype(BF16)
            return carry

        lax.fori_loop(0, 4, step, 0)

    def forward(m, t, out):
        ref = xb.at[m, t]
        factor = scale_of(ref)

        def down(o, total):
            for s in range(subs):
                normed = (ref[:, columns(o, s)].astype(F32) * factor).astype(BF16)
                total = total + dot(normed, wd[m, o, s * tile : (s + 1) * tile, :])
            return total

        latent = lax.fori_loop(0, 4, down, jnp.zeros((rows, wd.shape[3]), F32))
        active = (latent * jax.nn.sigmoid(latent)).astype(BF16)

        def up(o, carry):
            for s in range(subs):
                here = columns(o, s)
                branch = dot(active, wu[m, o, :, s * tile : (s + 1) * tile])
                out[:, here] = (ref[:, here].astype(F32) + branch).astype(BF16)
            return carry

        lax.fori_loop(0, 4, up, 0)

    def backward(m, t, out):
        ref = sv.at[m, t]
        incoming = gb.at[m, pl.ds(t * rows, rows)]
        zero = jnp.zeros((rows, wd.shape[3]), F32)

        def down(o, total):
            latent, d_active = total
            latent = latent + dot(ref[:, block(o)], wd[m, o])
            d_active = d_active + dot_nt(incoming[:, block(o)], wu[m, o])
            return latent, d_active

        latent, d_active = lax.fori_loop(0, 4, down, (zero, zero))
        squash = jax.nn.sigmoid(latent)
        active = latent * squash
        d_latent = (d_active * squash * (1.0 + latent * (1.0 - squash))).astype(BF16)
        dl[m, t * rows : (t + 1) * rows, :] = d_latent
        at[m, :, t * rows : (t + 1) * rows] = active.T.astype(BF16)
        inner = jnp.sum(d_latent.astype(F32) * latent, axis=1, keepdims=True) / width
        factor = sc[m, t][:, 0:1]

        def up(o, carry):
            for s in range(subs):
                here = columns(o, s)
                d_normed = dot_nt(d_latent, wd[m, o, s * tile : (s + 1) * tile, :])
                scaled = ref[:, here].astype(F32)
                out[:, here] = (
                    incoming[:, here].astype(F32) + factor * (d_normed - scaled * inner)
                ).astype(BF16)
            return carry

        lax.fori_loop(0, 4, up, 0)

    def pipe_copy(n):
        m = n % 2
        src = yb.at[m] if n < 2 else bb.at[m]
        dst = xb.at[m, 1] if n < 2 else gb.at[m, pl.ds(rows, rows)]
        return pltpu.make_async_remote_copy(
            src_ref=src,
            dst_ref=dst,
            send_sem=pp_s.at[n],
            recv_sem=pp_r.at[n],
            device_id=(p + 1 if n in (0, 3) else p - 1, d),
            device_id_type=MESH,
        )

    def pipe_ends(n):
        return (has_up, has_down) if n in (0, 3) else (has_down, has_up)

    def pipe_send(n, far):
        first = lax.rem(p, 2) == 0
        near = first if n in (0, 3) else jnp.logical_not(first)

        @pl.when(pipe_ends(n)[0] & (jnp.logical_not(near) if far else near))
        def _():
            pipe_copy(n).start()

    def pipe_wait(n):
        arrives = pipe_ends(n)[1]

        @pl.when(arrives)
        def _():
            pipe_copy(n).wait_recv()

        @pl.when(jnp.logical_not(arrives))
        def _():
            m = n % 2
            if n < 2:
                xb[m, 1] = jnp.zeros((rows, width), BF16)
            else:
                gb[m, rows : 2 * rows, :] = jnp.zeros((rows, width), BF16)

    def rs_copy(m, f, j, kind, target):
        held = (rsd, rsu)[kind]
        return pltpu.make_async_remote_copy(
            src_ref=held.at[f, m, j],
            dst_ref=held.at[f, m, j],
            send_sem=rs_s.at[f, m, j, kind],
            recv_sem=rs_r.at[f, m, j, kind],
            device_id=(p, target),
            device_id_type=MESH,
        )

    def operand(m, j, which):
        owner = jnp.where(d == 0, 3 - j, j)
        half = pl.ds(0 if which == 1 else rows, rows)
        src, dst = (
            (svt.at[m, block(owner)], far_n.at[m, j])
            if which == 0
            else (gb.at[m, half, block(owner)], far_g.at[m, j, half])
        )
        return pltpu.make_async_remote_copy(
            src_ref=src,
            dst_ref=dst,
            send_sem=op_s.at[m, j, which],
            recv_sem=op_r.at[m, j, which],
            device_id=(p, out_to),
            device_id_type=MESH,
        )

    def latents_copy(m, kind):
        return pltpu.make_async_remote_copy(
            src_ref=(dl, at)[kind].at[m],
            dst_ref=(far_dl, far_at)[kind].at[m],
            send_sem=lt_s.at[m, kind],
            recv_sem=lt_r.at[m, kind],
            device_id=(p, out_to),
            device_id_type=MESH,
        )

    def operand_from_end(m, j, which):
        @pl.when(is_end)
        def _():
            operand(m, j, which).start()

    def latents_from_end(m, kind):
        @pl.when(is_end)
        def _():
            latents_copy(m, kind).start()

    def latents_arrive(m):
        @pl.when(is_mid)
        def _():
            for kind in by_operands[m]:
                latents_copy(m, kind).wait_recv()

    def piece(m, o, kind, out, arrived=(), far=None):
        if far is not None:
            for which in ((0,), (1, 2))[kind]:
                operand(m, far, which).wait_recv()
        for s in range(subs):
            cut = slice(s * tile, (s + 1) * tile)
            if kind == 0:
                here = (cut, slice(None))
                part = dot(svt[m, columns(o, s), :], dl[m])
                if far is not None:
                    part = part + dot(far_n[m, far, cut, :], far_dl[m])
            else:
                here = (slice(None), cut)
                part = dot(at[m], gb[m, :, columns(o, s)])
                if far is not None:
                    part = part + dot(far_at[m], far_g[m, far, :, cut])
            for ref in arrived:
                part = part + ref[here].astype(F32)
            out[here] = part.astype(BF16)

    def grad_from_end(m, j, kind):
        @pl.when(is_end)
        def _():
            owner = jnp.where(d == 0, 3 - j, j)
            piece(m, owner, kind, (rsd, rsu)[kind].at[out_flow, m, j])
            rs_copy(m, out_flow, j, kind, out_to).start()

    def grad_across(m, j, kind):
        @pl.when(is_mid)
        def _():
            owner = jnp.where(d == 1, 3 - j, j)
            copy = rs_copy(m, cross_flow, j, kind, cross_to)
            held = (rsd, rsu)[kind].at[cross_flow, m, j]
            if kind in by_operands[m]:
                piece(m, owner, kind, held, (), j)
            else:
                copy.wait_recv()
                piece(m, owner, kind, held, (held,))
            copy.start()

    def grad_to_end(m, kind):
        @pl.when(is_mid)
        def _():
            copy = rs_copy(m, end_flow, 0, kind, end_to)
            copy.wait_recv()
            held = (rsd, rsu)[kind].at[end_flow, m, 0]
            piece(m, end_to, kind, held, (held,))
            copy.start()

    def grad_finish(m):
        for kind in range(2):
            held, out = (rsd, rsu)[kind], (gsd, gsu)[kind].at[m]

            @pl.when(is_end)
            def _():
                rs_copy(m, 1 - out_flow, 0, kind, out_to).wait_recv()
                piece(m, d, kind, out, (held.at[1 - out_flow, m, 0],))

            @pl.when(is_mid)
            def _():
                rs_copy(m, end_flow, 1, kind, end_to).wait_recv()
                if kind in by_operands[m]:
                    piece(m, d, kind, out, (held.at[end_flow, m, 1],), 2)
                else:
                    rs_copy(m, cross_flow, 2, kind, cross_to).wait_recv()
                    piece(m, d, kind, out, (held.at[cross_flow, m, 2], held.at[end_flow, m, 1]))

            result(4 + 2 * m + kind).start()

    results = (
        (ob.at[0], o_lf), (ob.at[1], o_mf), (ob.at[2], o_lb), (ob.at[3], o_mb),
        (gsd.at[0], o_ld), (gsu.at[0], o_lu), (gsd.at[1], o_md), (gsu.at[1], o_mu),
    )

    def result(n):
        return pltpu.make_async_copy(results[n][0], results[n][1].at[0], out_sem.at[n])

    own_to_end(0, 0)
    own_from_end(0, 0)
    own_from_end(0, 1)
    own_to_end(0, 1)
    own_from_end(1, 0)
    own_across(0, 1)
    loads["s", 1].wait()
    prepare(1, 1)
    own_across(0, 0)
    own_from_end(1, 1)
    pass_across(0, 0)
    prepare(1, 0)
    pass_to_end(0, 1, 1)
    pass_to_end(0, 0, 1)
    pass_across(0, 1)
    loads["s", 0].wait()
    prepare(0, 0)
    own_across(1, 1)
    pass_to_end(0, 0, 2)
    own_across(1, 0)
    operand_from_end(1, 2, 0)
    prepare(0, 1)
    pass_to_end(0, 1, 2)
    operand_from_end(1, 0, 0)
    own_to_end(1, 0)
    operand_from_end(1, 1, 0)
    loads["wd", 0].wait()
    loads["wu", 0].wait()
    loads["g", 0].wait()
    end_gathers(0)
    backward(0, 0, bb.at[0])
    pipe_send(2, True)
    pipe_send(2, False)
    pipe_wait(2)
    pass_across(1, 1)
    backward(0, 1, ob.at[2])
    result(2).start()
    pass_to_end(1, 0, 1)
    pass_across(1, 0)
    pass_to_end(1, 0, 2)
    pass_to_end(1, 1, 1)
    loads["x", 0].wait()
    forward(0, 0, yb.at[0])
    grad_from_end(0, 1, 0)
    own_to_end(1, 1)
    grad_across(0, 1, 0)
    grad_from_end(0, 0, 1)
    grad_from_end(0, 0, 0)
    grad_from_end(0, 1, 1)
    pass_to_end(1, 1, 2)
    grad_across(0, 0, 1)
    grad_from_end(0, 2, 1)
    loads["wd", 1].wait()
    loads["wu", 1].wait()
    loads["g", 1].wait()
    end_gathers(1)
    backward(1, 0, bb.at[1])
    loads["x", 1].wait()
    forward(1, 0, yb.at[1])
    pipe_send(1, True)
    grad_across(0, 0, 0)
    pipe_send(3, False)
    pipe_send(3, True)
    grad_across(0, 1, 1)
    pipe_send(0, True)
    pipe_wait(3)
    backward(1, 1, ob.at[3])
    result(3).start()
    latents_from_end(1, 0)
    pipe_send(1, False)
    latents_arrive(1)
    grad_from_end(1, 0, 1)
    grad_to_end(0, 1)
    grad_to_end(0, 0)
    grad_across(1, 0, 0)
    grad_from_end(1, 1, 1)
    pipe_send(0, False)
    grad_across(1, 0, 1)
    grad_to_end(1, 0)
    grad_across(1, 1, 0)
    grad_from_end(0, 2, 0)
    grad_to_end(1, 1)
    grad_across(1, 1, 1)
    pipe_wait(1)
    forward(1, 1, ob.at[1])
    result(1).start()
    grad_from_end(1, 2, 1)
    grad_finish(0)
    pipe_wait(0)
    forward(0, 1, ob.at[0])
    result(0).start()
    grad_finish(1)

    for m in range(2):
        for kind in range(2):

            @pl.when(is_end)
            def _(m=m, kind=kind):
                ag_copy(m, kind, out_flow, 0, d, out_to, True).wait_send()
                for j in range(3):
                    if kind in by_operands[m]:
                        for which in ((0,), (1, 2))[kind]:
                            operand(m, j, which).wait_send()
                    else:
                        rs_copy(m, out_flow, j, kind, out_to).wait_send()
                if kind in by_operands[m]:
                    latents_copy(m, kind).wait_send()

            @pl.when(is_mid)
            def _(m=m, kind=kind):
                for step in range(2):
                    ag_copy(m, kind, cross_flow, step, d, cross_to).wait_send()
                    rs_copy(m, cross_flow, step, kind, cross_to).wait_send()
                for step in range(3):
                    ag_copy(m, kind, end_flow, step, d, end_to).wait_send()
                rs_copy(m, end_flow, 0, kind, end_to).wait_send()

    for n in range(4):

        @pl.when(pipe_ends(n)[0])
        def _(n=n):
            pipe_copy(n).wait_send()

    for n in range(8):
        result(n).wait()


def body(*arrays):
    lf, ls, ld, lu = arrays[0], arrays[4], arrays[6], arrays[7]
    _, ticks, rows, width = ls.shape
    _, shard, latents = ld.shape
    outs = [jax.ShapeDtypeStruct(lf.shape, BF16)] * 4 + [
        jax.ShapeDtypeStruct(ld.shape, BF16),
        jax.ShapeDtypeStruct(lu.shape, BF16),
    ] * 2
    vmem = pltpu.VMEM
    dma = pltpu.SemaphoreType.DMA
    return pl.pallas_call(
        kernel,
        out_shape=outs,
        in_specs=[pl.BlockSpec(memory_space=pl.ANY)] * 10,
        out_specs=[pl.BlockSpec(memory_space=pl.ANY)] * 8,
        scratch_shapes=[
            vmem((2, 4, shard, latents), BF16),
            vmem((2, 4, latents, shard), BF16),
            vmem((2, ticks, rows, width), BF16),
            vmem((2, width, ticks * rows), BF16),
            vmem((2, ticks, rows, 128), F32),
            vmem((2, ticks * rows, width), BF16),
            vmem((2, ticks, rows, width), BF16),
            vmem((2, rows, width), BF16),
            vmem((2, rows, width), BF16),
            vmem((4, rows, width), BF16),
            vmem((2, ticks * rows, latents), BF16),
            vmem((2, latents, ticks * rows), BF16),
            vmem((2, 2, 3, shard, latents), BF16),
            vmem((2, 2, 3, latents, shard), BF16),
            vmem((2, shard, latents), BF16),
            vmem((2, latents, shard), BF16),
            vmem((2, 3, shard, ticks * rows), BF16),
            vmem((2, ticks * rows, latents), BF16),
            vmem((2, 3, ticks * rows, shard), BF16),
            vmem((2, latents, ticks * rows), BF16),
            dma((10,)),
            dma((8,)),
            dma((2, 2, 2, 3)),
            dma((2, 2, 2, 3)),
            dma((4,)),
            dma((4,)),
            dma((2, 2, 3, 2)),
            dma((2, 2, 3, 2)),
            dma((2, 3, 3)),
            dma((2, 3, 3)),
            dma((2, 2)),
            dma((2, 2)),
        ],
        compiler_params=pltpu.CompilerParams(
            collective_id=0, has_side_effects=True, vmem_limit_bytes=52 * 2**20
        ),
        name="relay_window",
    )(*arrays)


def solution(mesh):
    front = P("pipe", "dp", None)
    up = P("pipe", None, "dp")
    placed = (front,) * 4 + (P("pipe", None, "dp", None),) * 2 + (front, up, front, up)
    return jax.shard_map(
        body,
        mesh=mesh,
        in_specs=placed,
        out_specs=(front,) * 4 + (front, up, front, up),
        check_vma=False,
    )
```

```python
import functools

import jax
import jax.numpy as jnp
from jax import lax
from jax.experimental import pallas as pl
from jax.experimental.pallas import tpu as pltpu
from jax.sharding import PartitionSpec as P

EPS = 1e-06
MESH = pl.DeviceIdType.MESH
BF16 = jnp.bfloat16
F32 = jnp.float32
NT = (((1,), (1,)), ((), ()))


def dot(a, b):
    return jnp.dot(a, b, preferred_element_type=F32)


def dot_nt(a, b):
    return lax.dot_general(a, b, NT, preferred_element_type=F32)


def kernel(
    lf, mf, lg, mg, ls, ms, ld, lu, md, mu,
    o_lf, o_mf, o_lb, o_mb, o_ld, o_lu, o_md, o_mu,
    wd, wu, sv, svt, sc, gb, xb, yb, bb, ob, dl, at, rsd, rsu, gsd, gsu, far_n, far_dl, far_g, far_at,
    in_sem, out_sem, ag_s, ag_r, pp_s, pp_r, rs_s, rs_r, op_s, op_r, lt_s, lt_r,
):
    p, d = lax.axis_index("pipe"), lax.axis_index("dp")
    stages = lax.axis_size("pipe")
    _, _, rows, width = sv.shape
    shard = wd.shape[2]
    tile = min(256, shard)
    subs = shard // tile
    fronts, grads, saved = (lf, mf), (lg, mg), (ls, ms)
    downs, ups = (ld, md), (lu, mu)
    has_up, has_down = p < stages - 1, p > 0
    has_right, has_left = d < 3, d > 0
    is_end = (d == 0) | (d == 3)
    is_mid = (d == 1) | (d == 2)
    by_operands = ((), (0,))

    def local(src, dst, n):
        return pltpu.make_async_copy(src, dst, in_sem.at[n])

    loads = {}
    for m in range(2):
        loads["s", m] = local(saved[m].at[0], sv.at[m], m)
        loads["wd", m] = local(downs[m].at[0], wd.at[m, d], 2 + m)
        loads["wu", m] = local(ups[m].at[0], wu.at[m, d], 4 + m)
        loads["g", m] = local(grads[m].at[0], gb.at[m, pl.ds(0, rows)], 6 + m)
        loads["x", m] = local(fronts[m].at[0], xb.at[m, 0], 8 + m)
    for copy in loads.values():
        copy.start()

    barrier = pltpu.get_barrier_semaphore()
    around = (
        (has_up, (p + 1, d)),
        (has_down, (p - 1, d)),
        (has_right, (p, d + 1)),
        (has_left, (p, d - 1)),
    )
    for here, where in around:

        @pl.when(here)
        def _(where=where):
            pl.semaphore_signal(barrier, inc=1, device_id=where, device_id_type=MESH)

    pl.semaphore_wait(barrier, sum(here.astype(jnp.int32) for here, _ in around))

    out_to, out_flow = jnp.where(d == 0, 1, 2), jnp.where(d == 0, 0, 1)
    cross_to, cross_flow = 3 - d, jnp.clip(d - 1, 0, 1)
    end_to, end_flow = jnp.where(d == 1, 0, 3), jnp.clip(2 - d, 0, 1)

    def ag_copy(m, kind, flow, step, shard_of, target, own=False):
        whole = (wd, wu)[kind]
        return pltpu.make_async_remote_copy(
            src_ref=(downs, ups)[kind][m].at[0] if own else whole.at[m, shard_of],
            dst_ref=whole.at[m, shard_of],
            send_sem=ag_s.at[flow, m, kind, step],
            recv_sem=ag_r.at[flow, m, kind, step],
            device_id=(p, target),
            device_id_type=MESH,
        )

    def own_from_end(m, kind):
        @pl.when(is_end)
        def _():
            ag_copy(m, kind, out_flow, 0, d, out_to, True).start()

    def own_across(m, kind):
        @pl.when(is_mid)
        def _():
            ag_copy(m, kind, cross_flow, 0, d, cross_to, True).start()

    def own_to_end(m, kind):
        @pl.when(is_mid)
        def _():
            ag_copy(m, kind, end_flow, 0, d, end_to, True).start()

    def pass_across(m, kind):
        @pl.when(is_mid)
        def _():
            ag_copy(m, kind, cross_flow, 0, end_to, cross_to).wait_recv()
            ag_copy(m, kind, cross_flow, 1, end_to, cross_to).start()

    def pass_to_end(m, kind, step):
        shard_of = cross_to if step == 1 else 3 - end_to

        @pl.when(is_mid)
        def _():
            ag_copy(m, kind, end_flow, step - 1, shard_of, end_to).wait_recv()
            ag_copy(m, kind, end_flow, step, shard_of, end_to).start()

    def end_gathers(m):
        @pl.when(is_end)
        def _():
            for step in range(3):
                shard_of = jnp.where(d == 0, 1 + step, 2 - step)
                for kind in range(2):
                    ag_copy(m, kind, 1 - out_flow, step, shard_of, out_to).wait_recv()

    def columns(o, s):
        return pl.ds(pl.multiple_of(o * shard + s * tile, tile), tile)

    def block(o):
        return pl.ds(pl.multiple_of(o * shard, shard), shard)

    def scale_of(ref):
        def add(o, total):
            for s in range(subs):
                x = ref[:, columns(o, s)].astype(F32)
                total = total + x * x
            return total

        total = lax.fori_loop(0, 4, add, jnp.zeros((rows, tile), F32))
        return lax.rsqrt(jnp.sum(total, axis=1, keepdims=True) / width + EPS)

    def prepare(m, t):
        ref = sv.at[m, t]
        factor = scale_of(ref)
        sc[m, t] = jnp.broadcast_to(factor, (rows, 128))

        def step(o, carry):
            for s in range(subs):
                here = columns(o, s)
                normed = ref[:, here].astype(F32) * factor
                ref[:, here] = normed.astype(BF16)
                svt[m, here, t * rows : (t + 1) * rows] = normed.T.astype(BF16)
            return carry

        lax.fori_loop(0, 4, step, 0)

    def forward(m, t, out):
        ref = xb.at[m, t]
        factor = scale_of(ref)

        def down(o, total):
            for s in range(subs):
                normed = (ref[:, columns(o, s)].astype(F32) * factor).astype(BF16)
                total = total + dot(normed, wd[m, o, s * tile : (s + 1) * tile, :])
            return total

        latent = lax.fori_loop(0, 4, down, jnp.zeros((rows, wd.shape[3]), F32))
        active = (latent * jax.nn.sigmoid(latent)).astype(BF16)

        def up(o, carry):
            for s in range(subs):
                here = columns(o, s)
                branch = dot(active, wu[m, o, :, s * tile : (s + 1) * tile])
                out[:, here] = (ref[:, here].astype(F32) + branch).astype(BF16)
            return carry

        lax.fori_loop(0, 4, up, 0)

    def backward(m, t, out):
        ref = sv.at[m, t]
        incoming = gb.at[m, pl.ds(t * rows, rows)]
        zero = jnp.zeros((rows, wd.shape[3]), F32)

        def down(o, total):
            latent, d_active = total
            latent = latent + dot(ref[:, block(o)], wd[m, o])
            d_active = d_active + dot_nt(incoming[:, block(o)], wu[m, o])
            return latent, d_active

        latent, d_active = lax.fori_loop(0, 4, down, (zero, zero))
        squash = jax.nn.sigmoid(latent)
        active = latent * squash
        d_latent = (d_active * squash * (1.0 + latent * (1.0 - squash))).astype(BF16)
        dl[m, t * rows : (t + 1) * rows, :] = d_latent
        at[m, :, t * rows : (t + 1) * rows] = active.T.astype(BF16)
        inner = jnp.sum(d_latent.astype(F32) * latent, axis=1, keepdims=True) / width
        factor = sc[m, t][:, 0:1]

        def up(o, carry):
            for s in range(subs):
                here = columns(o, s)
                d_normed = dot_nt(d_latent, wd[m, o, s * tile : (s + 1) * tile, :])
                scaled = ref[:, here].astype(F32)
                out[:, here] = (
                    incoming[:, here].astype(F32) + factor * (d_normed - scaled * inner)
                ).astype(BF16)
            return carry

        lax.fori_loop(0, 4, up, 0)

    def pipe_copy(n):
        m = n % 2
        src = yb.at[m] if n < 2 else bb.at[m]
        dst = xb.at[m, 1] if n < 2 else gb.at[m, pl.ds(rows, rows)]
        return pltpu.make_async_remote_copy(
            src_ref=src,
            dst_ref=dst,
            send_sem=pp_s.at[n],
            recv_sem=pp_r.at[n],
            device_id=(p + 1 if n in (0, 3) else p - 1, d),
            device_id_type=MESH,
        )

    def pipe_ends(n):
        return (has_up, has_down) if n in (0, 3) else (has_down, has_up)

    def pipe_send(n, far):
        first = lax.rem(p, 2) == 0
        near = first if n in (0, 3) else jnp.logical_not(first)

        @pl.when(pipe_ends(n)[0] & (jnp.logical_not(near) if far else near))
        def _():
            pipe_copy(n).start()

    def pipe_wait(n):
        arrives = pipe_ends(n)[1]

        @pl.when(arrives)
        def _():
            pipe_copy(n).wait_recv()

        @pl.when(jnp.logical_not(arrives))
        def _():
            m = n % 2
            if n < 2:
                xb[m, 1] = jnp.zeros((rows, width), BF16)
            else:
                gb[m, rows : 2 * rows, :] = jnp.zeros((rows, width), BF16)

    def rs_copy(m, f, j, kind, target):
        held = (rsd, rsu)[kind]
        return pltpu.make_async_remote_copy(
            src_ref=held.at[f, m, j],
            dst_ref=held.at[f, m, j],
            send_sem=rs_s.at[f, m, j, kind],
            recv_sem=rs_r.at[f, m, j, kind],
            device_id=(p, target),
            device_id_type=MESH,
        )

    def operand(m, j, which):
        owner = jnp.where(d == 0, 3 - j, j)
        half = pl.ds(0 if which == 1 else rows, rows)
        src, dst = (
            (svt.at[m, block(owner)], far_n.at[m, j])
            if which == 0
            else (gb.at[m, half, block(owner)], far_g.at[m, j, half])
        )
        return pltpu.make_async_remote_copy(
            src_ref=src,
            dst_ref=dst,
            send_sem=op_s.at[m, j, which],
            recv_sem=op_r.at[m, j, which],
            device_id=(p, out_to),
            device_id_type=MESH,
        )

    def latents_copy(m, kind):
        return pltpu.make_async_remote_copy(
            src_ref=(dl, at)[kind].at[m],
            dst_ref=(far_dl, far_at)[kind].at[m],
            send_sem=lt_s.at[m, kind],
            recv_sem=lt_r.at[m, kind],
            device_id=(p, out_to),
            device_id_type=MESH,
        )

    def operand_from_end(m, j, which):
        @pl.when(is_end)
        def _():
            operand(m, j, which).start()

    def latents_from_end(m, kind):
        @pl.when(is_end)
        def _():
            latents_copy(m, kind).start()

    def latents_arrive(m):
        @pl.when(is_mid)
        def _():
            for kind in by_operands[m]:
                latents_copy(m, kind).wait_recv()

    def piece(m, o, kind, out, arrived=(), far=None):
        if far is not None:
            for which in ((0,), (1, 2))[kind]:
                operand(m, far, which).wait_recv()
        for s in range(subs):
            cut = slice(s * tile, (s + 1) * tile)
            if kind == 0:
                here = (cut, slice(None))
                part = dot(svt[m, columns(o, s), :], dl[m])
                if far is not None:
                    part = part + dot(far_n[m, far, cut, :], far_dl[m])
            else:
                here = (slice(None), cut)
                part = dot(at[m], gb[m, :, columns(o, s)])
                if far is not None:
                    part = part + dot(far_at[m], far_g[m, far, :, cut])
            for ref in arrived:
                part = part + ref[here].astype(F32)
            out[here] = part.astype(BF16)

    def grad_from_end(m, j, kind):
        @pl.when(is_end)
        def _():
            owner = jnp.where(d == 0, 3 - j, j)
            piece(m, owner, kind, (rsd, rsu)[kind].at[out_flow, m, j])
            rs_copy(m, out_flow, j, kind, out_to).start()

    def grad_across(m, j, kind):
        @pl.when(is_mid)
        def _():
            owner = jnp.where(d == 1, 3 - j, j)
            copy = rs_copy(m, cross_flow, j, kind, cross_to)
            held = (rsd, rsu)[kind].at[cross_flow, m, j]
            if kind in by_operands[m]:
                piece(m, owner, kind, held, (), j)
            else:
                copy.wait_recv()
                piece(m, owner, kind, held, (held,))
            copy.start()

    def grad_to_end(m, kind):
        @pl.when(is_mid)
        def _():
            copy = rs_copy(m, end_flow, 0, kind, end_to)
            copy.wait_recv()
            held = (rsd, rsu)[kind].at[end_flow, m, 0]
            piece(m, end_to, kind, held, (held,))
            copy.start()

    def grad_finish(m):
        for kind in range(2):
            held, out = (rsd, rsu)[kind], (gsd, gsu)[kind].at[m]

            @pl.when(is_end)
            def _():
                rs_copy(m, 1 - out_flow, 0, kind, out_to).wait_recv()
                piece(m, d, kind, out, (held.at[1 - out_flow, m, 0],))

            @pl.when(is_mid)
            def _():
                rs_copy(m, end_flow, 1, kind, end_to).wait_recv()
                if kind in by_operands[m]:
                    piece(m, d, kind, out, (held.at[end_flow, m, 1],), 2)
                else:
                    rs_copy(m, cross_flow, 2, kind, cross_to).wait_recv()
                    piece(m, d, kind, out, (held.at[cross_flow, m, 2], held.at[end_flow, m, 1]))

            result(4 + 2 * m + kind).start()

    results = (
        (ob.at[0], o_lf), (ob.at[1], o_mf), (ob.at[2], o_lb), (ob.at[3], o_mb),
        (gsd.at[0], o_ld), (gsu.at[0], o_lu), (gsd.at[1], o_md), (gsu.at[1], o_mu),
    )

    def result(n):
        return pltpu.make_async_copy(results[n][0], results[n][1].at[0], out_sem.at[n])

    own_to_end(0, 0)
    own_from_end(0, 0)
    own_from_end(0, 1)
    own_to_end(0, 1)
    own_from_end(1, 0)
    own_across(0, 1)
    loads["s", 1].wait()
    prepare(1, 1)
    own_across(0, 0)
    own_from_end(1, 1)
    pass_across(0, 0)
    prepare(1, 0)
    pass_to_end(0, 1, 1)
    pass_to_end(0, 0, 1)
    pass_across(0, 1)
    loads["s", 0].wait()
    prepare(0, 0)
    own_across(1, 1)
    pass_to_end(0, 0, 2)
    own_across(1, 0)
    operand_from_end(1, 2, 0)
    prepare(0, 1)
    pass_to_end(0, 1, 2)
    operand_from_end(1, 0, 0)
    own_to_end(1, 0)
    operand_from_end(1, 1, 0)
    loads["wd", 0].wait()
    loads["wu", 0].wait()
    loads["g", 0].wait()
    end_gathers(0)
    backward(0, 0, bb.at[0])
    pipe_send(2, True)
    pipe_send(2, False)
    pipe_wait(2)
    pass_across(1, 1)
    backward(0, 1, ob.at[2])
    result(2).start()
    pass_to_end(1, 0, 1)
    pass_across(1, 0)
    pass_to_end(1, 0, 2)
    pass_to_end(1, 1, 1)
    loads["x", 0].wait()
    forward(0, 0, yb.at[0])
    grad_from_end(0, 1, 0)
    own_to_end(1, 1)
    grad_across(0, 1, 0)
    grad_from_end(0, 0, 1)
    grad_from_end(0, 0, 0)
    grad_from_end(0, 1, 1)
    pass_to_end(1, 1, 2)
    grad_across(0, 0, 1)
    grad_from_end(0, 2, 1)
    loads["wd", 1].wait()
    loads["wu", 1].wait()
    loads["g", 1].wait()
    end_gathers(1)
    backward(1, 0, bb.at[1])
    loads["x", 1].wait()
    forward(1, 0, yb.at[1])
    pipe_send(1, True)
    grad_across(0, 0, 0)
    pipe_send(3, False)
    pipe_send(3, True)
    grad_across(0, 1, 1)
    pipe_send(0, True)
    pipe_wait(3)
    backward(1, 1, ob.at[3])
    result(3).start()
    latents_from_end(1, 0)
    pipe_send(1, False)
    latents_arrive(1)
    grad_from_end(1, 0, 1)
    grad_to_end(0, 1)
    grad_to_end(0, 0)
    grad_across(1, 0, 0)
    grad_from_end(1, 1, 1)
    pipe_send(0, False)
    grad_across(1, 0, 1)
    grad_to_end(1, 0)
    grad_across(1, 1, 0)
    grad_from_end(0, 2, 0)
    grad_to_end(1, 1)
    grad_across(1, 1, 1)
    pipe_wait(1)
    forward(1, 1, ob.at[1])
    result(1).start()
    grad_from_end(1, 2, 1)
    grad_finish(0)
    pipe_wait(0)
    forward(0, 1, ob.at[0])
    result(0).start()
    grad_finish(1)

    for m in range(2):
        for kind in range(2):

            @pl.when(is_end)
            def _(m=m, kind=kind):
                ag_copy(m, kind, out_flow, 0, d, out_to, True).wait_send()
                for j in range(3):
                    if kind in by_operands[m]:
                        for which in ((0,), (1, 2))[kind]:
                            operand(m, j, which).wait_send()
                    else:
                        rs_copy(m, out_flow, j, kind, out_to).wait_send()
                if kind in by_operands[m]:
                    latents_copy(m, kind).wait_send()

            @pl.when(is_mid)
            def _(m=m, kind=kind):
                for step in range(2):
                    ag_copy(m, kind, cross_flow, step, d, cross_to).wait_send()
                    rs_copy(m, cross_flow, step, kind, cross_to).wait_send()
                for step in range(3):
                    ag_copy(m, kind, end_flow, step, d, end_to).wait_send()
                rs_copy(m, end_flow, 0, kind, end_to).wait_send()

    for n in range(4):

        @pl.when(pipe_ends(n)[0])
        def _(n=n):
            pipe_copy(n).wait_send()

    for n in range(8):
        result(n).wait()


def hand_over(*refs):
    for source, target in zip(refs[:8], refs[8:]):
        target[...] = source[...]


def body(*arrays):
    lf, ls, ld, lu = arrays[0], arrays[4], arrays[6], arrays[7]
    _, ticks, rows, width = ls.shape
    _, shard, latents = ld.shape
    outs = [jax.ShapeDtypeStruct(lf.shape, BF16)] * 4 + [
        jax.ShapeDtypeStruct(ld.shape, BF16),
        jax.ShapeDtypeStruct(lu.shape, BF16),
    ] * 2
    vmem = pltpu.VMEM
    dma = pltpu.SemaphoreType.DMA
    results = pl.pallas_call(
        kernel,
        out_shape=outs,
        in_specs=[pl.BlockSpec(memory_space=pl.ANY)] * 10,
        out_specs=[pl.BlockSpec(memory_space=pl.ANY)] * 8,
        scratch_shapes=[
            vmem((2, 4, shard, latents), BF16),
            vmem((2, 4, latents, shard), BF16),
            vmem((2, ticks, rows, width), BF16),
            vmem((2, width, ticks * rows), BF16),
            vmem((2, ticks, rows, 128), F32),
            vmem((2, ticks * rows, width), BF16),
            vmem((2, ticks, rows, width), BF16),
            vmem((2, rows, width), BF16),
            vmem((2, rows, width), BF16),
            vmem((4, rows, width), BF16),
            vmem((2, ticks * rows, latents), BF16),
            vmem((2, latents, ticks * rows), BF16),
            vmem((2, 2, 3, shard, latents), BF16),
            vmem((2, 2, 3, latents, shard), BF16),
            vmem((2, shard, latents), BF16),
            vmem((2, latents, shard), BF16),
            vmem((2, 3, shard, ticks * rows), BF16),
            vmem((2, ticks * rows, latents), BF16),
            vmem((2, 3, ticks * rows, shard), BF16),
            vmem((2, latents, ticks * rows), BF16),
            dma((10,)),
            dma((8,)),
            dma((2, 2, 2, 3)),
            dma((2, 2, 2, 3)),
            dma((4,)),
            dma((4,)),
            dma((2, 2, 3, 2)),
            dma((2, 2, 3, 2)),
            dma((2, 3, 3)),
            dma((2, 3, 3)),
            dma((2, 2)),
            dma((2, 2)),
        ],
        compiler_params=pltpu.CompilerParams(
            collective_id=0, has_side_effects=True, vmem_limit_bytes=62 * 2**20
        ),
        name="relay_window",
    )(*arrays)
    parts = 2
    blocks = [
        pl.BlockSpec((1, out.shape[1] // parts, out.shape[2]), lambda n: (0, n, 0)) for out in outs
    ]
    return pl.pallas_call(
        hand_over,
        grid=(parts,),
        out_shape=outs,
        in_specs=blocks,
        out_specs=blocks,
        name="hand_over",
    )(*results)


def solution(mesh):
    front = P("pipe", "dp", None)
    up = P("pipe", None, "dp")
    placed = (front,) * 4 + (P("pipe", None, "dp", None),) * 2 + (front, up, front, up)
    return jax.shard_map(
        body,
        mesh=mesh,
        in_specs=placed,
        out_specs=(front,) * 4 + (front, up, front, up),
        check_vma=False,
    )
```
